128 devices in a mesh: row: 8 (over z_hi, x), col: 16 (over z_lo, y, core).
Axes of the slice: x: 4, y: 4, z: 4 (z_hi: 2, z_lo: 2; z = z_hi * 2 + z_lo), core: 2. Of those that a mesh axis runs over, the one named last changes fastest.
Arguments:
- depth: float32 [2048, 16384], P('row', 'col'), may hold values from 0.05 to 3
- flow_east: float32 [2048, 16384], P('row', 'col'), may hold values from -3 to 3
- flow_south: float32 [2048, 16384], P('row', 'col'), may hold values from -3 to 3
- elevation: float32 [2048, 16384], P('row', 'col'), may hold values from -3 to 3
- roughness: float32 [2048, 16384], P('row', 'col'), may hold values from 0.02 to 0.15
- wet_mask: int32 [2048, 16384], P('row', 'col'), may hold values 0 or 1
- rainfall: bfloat16 [2, 3, 2048, 16384], P(None, None, ('row', 'col')), may hold values from 0.0019989014 to 0.049804688
- panel_source: int32 [256, 128], P('row', 'col'), may hold values from 0 to 2
- inflow: float32 [32768, 128], P(('row', 'col')), may hold values from 0.01 to 0.2
- gauge_tile: int32 [32768, 1], P(('row', 'col')), may hold values from 0 to 127; in each aligned block of 256 rows (0 to 255, 256 to 511, ...) at most 4 rows name the same one
- gauge_cell: int32 [32768], P(('row', 'col')), may hold values from 0 to 2047
Outputs:
- depth_out: float32 [2048, 16384], P('row', 'col')
- east_out: float32 [2048, 16384], P('row', 'col')
- south_out: float32 [2048, 16384], P('row', 'col')
The draws below stay inside these ranges and needn't reach their ends.
Inputs may be any that keep to these rules, and one draw needn't show every extreme that they name: `gauge_tile`: among the gauges of one device no tile is named more than 4 times, a bound that some block reaches.
All inputs are finite; a program needn't handle non-finite values. No bound on the sum of `wet_mask` on one device may be relied on, other than what follows from the above.
Results may differ from the reference program's by a relative error of at most 0.0003.
Values may be sent and summed in bfloat16 or wider, within the bound.
A program may use at most 192 MiB of HBM per device.

```python
import math
import jax
import jax.numpy as jnp
import numpy as np

TR = 256
TC = 1024
STEPS = 20
FRAMES = 2
SOURCES = 3
PANEL_ROWS = 8
BLOCK = 128
CAP = 4
G_DEV = 256
GAUGES = 32768
NR = 2048
NC = 16384
N_COL = 16
DEVICES = 128


def place_ends(values, key, least, largest):
    spot = [jax.random.randint(jax.random.fold_in(key, axis), (), 0, length) for axis, length in enumerate(values.shape)]
    main_axis = values.shape.index(max(values.shape))
    beside = spot[:main_axis] + [(spot[main_axis] + 1) % values.shape[main_axis]] + spot[main_axis + 1:]
    return values.at[tuple(spot)].set(least).at[tuple(beside)].set(largest)


def level_of(key, extent, split, smallest, high):
    factor_of = 1.0
    for axis_at, shards_of in split:
        draws = jax.random.uniform(jax.random.fold_in(jax.random.fold_in(key, 6), axis_at), (shards_of,), jnp.float32, smallest / len(split), high / len(split))
        factor_of = factor_of * jnp.repeat(jnp.exp(draws), extent[axis_at] // shards_of).reshape((-1,) + (1,) * (len(extent) - 1 - axis_at))
    return factor_of


def shared_out(key, own, number, rows, number_of, top, bound, lean):
    ranking = jax.random.permutation(key, number_of)
    heavy_load, common = load_shares(number_of, rows * top, bound, lean, True), load_shares(number_of, rows * top, bound, lean, False)
    places = jnp.arange(number_of)

    def named(sizes, turn):
        used = int((sizes > 0).sum())
        fixed = max(1, used // 4)
        shifted = fixed + (places - fixed + turn * (used - fixed)) % max(1, number_of - fixed)
        return jnp.zeros((number_of,), jnp.int32).at[ranking[jnp.where(places < fixed, places, shifted)]].set(jnp.asarray(sizes, jnp.int32))

    sizes = jnp.where(number % 4 == 0, named(heavy_load, number // 4), named(common, number - number // 4 - 1))
    mixed = jax.random.permutation(jax.random.fold_in(own, 3), number_of)
    source_of, sink = mixed[0:number_of // 2 * 2:2], mixed[1:number_of // 2 * 2:2]
    slack = jnp.minimum(sizes[source_of] - 1, bound - sizes[sink]) // 2
    slack = jnp.where((source_of == ranking[0]) | (sink == ranking[0]) | (sizes[sink] == 0), 0, jnp.maximum(slack, 0))
    shifted = jax.random.randint(jax.random.fold_in(own, 4), (number_of // 2,), 0, 1 << 20) % (slack + 1)
    sizes = sizes.at[source_of].add(-shifted).at[sink].add(shifted)
    labels = jnp.searchsorted(jnp.cumsum(sizes), jnp.arange(rows * top), side="right").astype(jnp.int32)
    listing = labels.reshape(top, rows).T
    listing = listing[jax.random.permutation(jax.random.fold_in(own, 1), rows)]
    turn = jax.random.randint(jax.random.fold_in(own, 2), (rows, 1), 0, top)
    return jnp.take_along_axis(listing, (jnp.arange(top)[None, :] + turn) % top, axis=1)


def load_shares(amount, total, bound, lean, full):
    weights = [(1 << 20) // math.isqrt(grade ** lean) + 1 for grade in range(1, amount + 1)]
    largest = bound if full else min(bound, max(-(-total // amount), total * weights[0] // sum(weights)))
    least = 1 if total - largest >= amount - 1 else 0
    holding, rest = [largest] + [least] * (amount - 1), total - largest - least * (amount - 1)
    while rest > 0:
        movable = [i for i in range(1, amount) if holding[i] < largest] or [i for i in range(1, amount) if holding[i] < bound]
        mass, remaining = sum([weights[i] for i in movable]), rest
        for i in movable:
            more = min(bound - holding[i], max(1, remaining * weights[i] // mass), rest)
            holding[i] = holding[i] + more
            rest = rest - more
    return np.array(holding)


def noise(key, dims, scale, reach, cuts=(), dtype=jnp.bfloat16):
    drawn = jax.random.normal(key, dims, jnp.float32) * scale
    if len(cuts) > 0:
        drawn = level_of(key, dims, cuts, -0.22, 0.18) * drawn
    return jnp.clip(drawn, min=-reach, max=reach).astype(dtype)


def setup_inputs(seed: int = 0) -> dict:
    arg_keys = jax.random.split(jax.random.key(seed), 12)
    depth = jnp.clip(jnp.exp(math.log(3.0) - 4.0943445 * jax.random.uniform(arg_keys[0], (NR, NC), jnp.float32) ** level_of(arg_keys[0], (NR, NC), ((0, 8), (1, 16)), -0.2, 0.2)), 0.05, 3.0)
    flow_east = noise(arg_keys[1], (NR, NC), 0.5, 3.0, ((0, 8), (1, 16)), jnp.float32)
    flow_south = noise(arg_keys[2], (NR, NC), 0.5, 3.0, ((0, 8), (1, 16)), jnp.float32)
    elevation = noise(arg_keys[3], (NR, NC), 0.6, 3.0, ((0, 8), (1, 16)), jnp.float32)
    roughness = jnp.clip(jnp.exp(math.log(0.15) - 2.014903 * jax.random.uniform(arg_keys[4], (NR, NC), jnp.float32) ** level_of(arg_keys[4], (NR, NC), ((0, 8), (1, 16)), -0.2, 0.2)), 0.02, 0.15)
    wet_mask = place_ends((jax.random.randint(arg_keys[5], (NR, NC), 0, 8) < 7).astype(jnp.int32), jax.random.fold_in(arg_keys[5], 1), 0, 1)
    rainfall = jnp.clip(jnp.exp(math.log(0.049804688) - 3.2155114 * jax.random.uniform(arg_keys[6], (FRAMES, SOURCES, NR, NC), jnp.float32) ** level_of(arg_keys[6], (FRAMES, SOURCES, NR, NC), ((2, 128),), -0.2, 0.2)), 0.0019989014, 0.049804688).astype(jnp.bfloat16)
    panel_source = place_ends(jax.random.randint(arg_keys[7], (NR // PANEL_ROWS, NC // BLOCK), 0, SOURCES), jax.random.fold_in(arg_keys[7], 1), 0, SOURCES - 1).astype(jnp.int32)
    inflow = jnp.clip(jnp.exp(math.log(0.2) - 2.9957323 * jax.random.uniform(arg_keys[8], (GAUGES, BLOCK), jnp.float32) ** level_of(arg_keys[8], (GAUGES, BLOCK), ((0, 128),), -0.2, 0.2)), 0.01, 0.2)
    gauge_tile_keys = jax.random.split(jax.random.fold_in(arg_keys[9], 1), GAUGES // G_DEV)
    gauge_tile_turns = jax.random.permutation(jax.random.fold_in(arg_keys[9], 3), GAUGES // G_DEV)
    gauge_tile = jax.vmap(lambda own, number: shared_out(jax.random.fold_in(arg_keys[9], 2), own, number, G_DEV, DEVICES, 1, CAP, 2))(gauge_tile_keys, gauge_tile_turns).reshape((GAUGES, 1))
    gauge_cell = place_ends(jax.random.randint(arg_keys[10], (GAUGES,), 0, TR * (TC // BLOCK)), jax.random.fold_in(arg_keys[10], 1), 0, (TR * (TC // BLOCK)) - 1).astype(jnp.int32)
    return dict(depth=depth, flow_east=flow_east, flow_south=flow_south, elevation=elevation, roughness=roughness, wet_mask=wet_mask, rainfall=rainfall, panel_source=panel_source, inflow=inflow, gauge_tile=gauge_tile, gauge_cell=gauge_cell)


gravity = 9.81
time_step = 5.0
cell_size = 90.0
depth_floor = 0.1


def select_source(rain, source_map):
    frames, sources, rows, cols = rain.shape
    shaped = rain.reshape(frames, sources, rows // PANEL_ROWS, PANEL_ROWS, cols // BLOCK, BLOCK)
    picker = source_map[:, None, :, None]
    chosen = shaped[:, 0]
    for source in range(1, sources):
        chosen = jnp.where(picker == source, shaped[:, source], chosen)
    return chosen.reshape(frames, rows, cols)


def face_flow(flow, eta, eta_next, zmax, fric, opened):
    depth_face = jnp.maximum(jnp.maximum(eta, eta_next) - zmax, depth_floor)
    slope = (eta_next - eta) / cell_size
    driven = flow - gravity * depth_face * time_step * slope
    return opened * driven / (1.0 + fric * jnp.abs(flow) / jnp.power(depth_face, 7.0 / 3.0))


def east_of(field):
    return jnp.concatenate([field[:, 1:], jnp.zeros_like(field[:, :1])], 1)


def south_of(field):
    return jnp.concatenate([field[1:, :], jnp.zeros_like(field[:1, :])], 0)


def reference(depth, flow_east, flow_south, elevation, roughness, wet_mask, rainfall, panel_source, inflow, gauge_tile, gauge_cell):
    maskf = wet_mask.astype(jnp.float32)
    open_e = maskf * east_of(maskf)
    open_s = maskf * south_of(maskf)
    zmax_e = jnp.maximum(elevation, east_of(elevation))
    zmax_s = jnp.maximum(elevation, south_of(elevation))
    fric_e = gravity * time_step * jnp.square(0.5 * (roughness + east_of(roughness)))
    fric_s = gravity * time_step * jnp.square(0.5 * (roughness + south_of(roughness)))
    rain_sel = select_source(rainfall, panel_source)
    blocks_row = TC // BLOCK
    target = gauge_tile[:, 0].astype(jnp.int32)
    cell = gauge_cell.astype(jnp.int32)
    rows_at = (target // N_COL) * TR + cell // blocks_row
    cols_at = (target % N_COL) * blocks_row + cell % blocks_row
    source_in = jnp.zeros((NR, NC // BLOCK, BLOCK), jnp.float32).at[rows_at, cols_at].add(inflow).reshape(NR, NC)
    ratio = time_step / cell_size
    height = depth
    east_q = flow_east
    south_q = flow_south
    for step in range(STEPS):
        eta = height + elevation
        east_q = face_flow(east_q, eta, east_of(eta), zmax_e, fric_e, open_e)
        south_q = face_flow(south_q, eta, south_of(eta), zmax_s, fric_s, open_s)
        west_q = jnp.concatenate([jnp.zeros_like(east_q[:, :1]), east_q[:, :-1]], 1)
        north_q = jnp.concatenate([jnp.zeros_like(south_q[:1, :]), south_q[:-1, :]], 0)
        frame = step * FRAMES // STEPS
        height = height + ratio * ((west_q - east_q) + (north_q - south_q)) + (rain_sel[frame].astype(jnp.float32) + source_in)
    return height, east_q, south_q
```

```python
import functools

import jax
import jax.numpy as jnp
from jax import lax
from jax.experimental import pallas as pl
from jax.experimental.pallas import tpu as pltpu
from jax.sharding import PartitionSpec as P

STEPS = 20
FRAMES = 2
SOURCES = 3
PANEL_ROWS = 8
LANES = 128
CAP = 4
NR = 8
NCOL = 16
TR = 256
NB = 8
HALO = 24
BASE = 32
RP = 320
STRIPE = TR // NCOL
GD = 256
NX = 5

GRAVITY = 9.81
DT = 5.0
DX = 90.0
RATIO = DT / DX
SCALE = RATIO * GRAVITY * DT / DX
QSCALE = SCALE * RATIO
FLOOR = 0.1 * SCALE
FRIC = GRAVITY * DT * 0.25 * SCALE ** (7.0 / 3.0) / QSCALE
MESH = pl.DeviceIdType.MESH


def split3(x):
    hi = x.astype(jnp.bfloat16)
    rest = x - hi.astype(jnp.float32)
    mid = rest.astype(jnp.bfloat16)
    low = (rest - mid.astype(jnp.float32)).astype(jnp.bfloat16)
    return jnp.concatenate([hi, mid, low], axis=1)


def join3(x):
    return (x[:, :LANES] + x[:, LANES : 2 * LANES]) + x[:, 2 * LANES :]


def dot(a, b):
    return lax.dot_general(a, b, (((1,), (0,)), ((), ())), preferred_element_type=jnp.float32)


def iota(shape, axis):
    return lax.broadcasted_iota(jnp.int32, shape, axis)


def face(eta, nxt, q, zmax, fric, base):
    hf = jnp.maximum(jnp.maximum(eta, nxt) - zmax, FLOOR)
    drv = q - hf * (nxt - eta)
    pw = jnp.exp2(jnp.log2(hf) * (-7.0 / 3.0))
    return drv * (1.0 / (base + jnp.abs(q) * fric * pw))


def mul8(x):
    return pl.multiple_of(x * 8, 8)


def kernel(
    depth, flow_e, flow_s, elev, rough, wet, rain, panel, inflow, gtile, gcell,
    out_h, out_e, out_s,
    stage, wet_v, rain_v, panel_v, inflow_v, gtile_v, gcell_v,
    X, ZE, ZS, FE, FS, BE, BS, EN, S, SG,
    panel_r, ga, ga_r, gb, gb_r, rs, rx, pack_l, pack_r, got_l, got_r, spack_l, spack_r, sgot_l, sgot_r, outs,
    loc, panel_ss, panel_rs, ga_ss, ga_rs, gb_ss, gb_rs, rain_ss, rain_rs,
    col_ss, col_rs, row_ss, row_rs, row8_ss, row8_rs,
    scol_ss, scol_rs, srow_ss, srow_rs, srow8_ss, srow8_rs,
):
    r = lax.axis_index("row")
    c = lax.axis_index("col")
    up, down = lax.rem(r + NR - 1, NR), lax.rem(r + 1, NR)
    left, right = lax.rem(c + NCOL - 1, NCOL), lax.rem(c + 1, NCOL)

    def local(src, dst, k):
        cp = pltpu.make_async_copy(src, dst, loc.at[k])
        cp.start()
        return cp

    def remote(src, dst, ss, rs_, dev):
        return pltpu.make_async_remote_copy(
            src_ref=src, dst_ref=dst, send_sem=ss, recv_sem=rs_, device_id=dev, device_id_type=MESH
        )

    in_panel = local(panel, panel_v, 0)
    in_gauge = [local(inflow, inflow_v, 1), local(gtile, gtile_v, 2), local(gcell, gcell_v, 3)]
    in_tile = [
        local(depth, stage.at[0], 4),
        local(flow_e, stage.at[1], 5),
        local(flow_s, stage.at[2], 6),
        local(elev, stage.at[3], 7),
        local(rough, stage.at[4], 8),
        local(wet, wet_v, 9),
    ]
    in_rain = [local(rain.at[f], rain_v.at[f], 10 + f) for f in range(FRAMES)]

    barrier = pltpu.get_barrier_semaphore()
    for o in range(1, NCOL):
        pl.semaphore_signal(barrier, inc=1, device_id=(r, lax.rem(c + o, NCOL)), device_id_type=MESH)
    for o in range(1, NR):
        pl.semaphore_signal(barrier, inc=1, device_id=(lax.rem(r + o, NR), c), device_id_type=MESH)
    pl.semaphore_wait(barrier, NCOL + NR - 2)

    in_panel.wait()
    panel_cp = []
    per_tile = STRIPE // PANEL_ROWS
    for o in range(1, NCOL):
        to = lax.rem(c + o, NCOL)
        rows = pl.ds(mul8(to * per_tile // 8), 8)
        cp = remote(panel_v.at[rows, :], panel_r.at[c], panel_ss.at[o], panel_rs.at[o], (r, to))
        cp.start()
        panel_cp.append(cp)
    panel_r[c] = panel_v[pl.ds(mul8(c * per_tile // 8), 8), :]

    for cp in in_gauge:
        cp.wait()
    g0, g1 = iota((GD, GD), 0), iota((GD, GD), 1)
    eye = g0 == g1
    tile_b = jnp.broadcast_to(gtile_v[...].astype(jnp.float32), (GD, GD))
    tile_row = jnp.sum(jnp.where(eye, tile_b, 0.0), axis=0, keepdims=True)
    same = tile_b == tile_row
    rank_col = jnp.sum(jnp.where(same & (g1 < g0), 1.0, 0.0), axis=1, keepdims=True)
    rank_row = jnp.sum(jnp.where(same & (g0 < g1), 1.0, 0.0), axis=0, keepdims=True)
    tile_r = jnp.floor(tile_row * (1.0 / NCOL))
    tile_c = tile_row - tile_r * NCOL
    slot = (tile_c * NR + tile_r) * CAP + rank_row
    slots = NR * NCOL * CAP
    pick = jnp.where(iota((slots, GD), 0).astype(jnp.float32) == slot, 1.0, 0.0).astype(jnp.bfloat16)
    vals = join3(dot(pick, split3(inflow_v[...])))
    cells = jnp.concatenate([gcell_v[k : k + 1, :] for k in range(GD // LANES)], axis=1).astype(jnp.float32)
    cell_col = jnp.sum(jnp.where(eye, cells, 0.0), axis=1, keepdims=True)
    cell_hi = jnp.floor(cell_col * 0.125)
    cell_lo = cell_col - cell_hi * 8.0
    mine = rank_col == lax.rem(iota((GD, LANES), 1), CAP).astype(jnp.float32)
    cell_x = jnp.concatenate([jnp.where(mine, cell_hi, 0.0), jnp.where(mine, cell_lo, 0.0)], axis=1)
    order = iota((NR * NCOL, GD), 0).astype(jnp.float32) == tile_c * NR + tile_r
    cell_y = dot(jnp.where(order, 1.0, 0.0).astype(jnp.bfloat16), cell_x.astype(jnp.bfloat16))
    cell_t = cell_y[:, :LANES] * 8.0 + cell_y[:, LANES:]
    per = NR * CAP
    for k in range(NCOL):
        ga[k, 8 : 8 + per, :] = vals[k * per : (k + 1) * per]
        ga[k, 8 + per : 16 + per, :] = cell_t[k * NR : (k + 1) * NR]
    ga_cp = []
    for o in range(1, NCOL):
        to = lax.rem(c + o, NCOL)
        cp = remote(
            ga.at[to, pl.ds(8, per + 8)], ga_r.at[c, pl.ds(8, per + 8)], ga_ss.at[o], ga_rs.at[o], (r, to)
        )
        cp.start()
        ga_cp.append(cp)
    ga_r[c, pl.ds(8, per + 8), :] = ga[c, pl.ds(8, per + 8), :]

    for cp in in_tile:
        cp.wait()

    def scale_rows(i, _):
        rows = pl.ds(mul8(i), 8)
        to = pl.ds(mul8(i + BASE // 8), 8)
        for b in range(NB):
            cols = pl.ds(b * LANES, LANES)
            z = stage[3, rows, cols] * SCALE
            X[0, b, to, :] = stage[0, rows, cols] * SCALE + z
            X[1, b, to, :] = stage[1, rows, cols] * QSCALE
            X[2, b, to, :] = stage[2, rows, cols] * QSCALE
            X[3, b, to, :] = z
            n = stage[4, rows, cols]
            X[4, b, to, :] = jnp.where(wet_v[rows, cols] > 0, n, -n)
        return 0

    lax.fori_loop(0, TR // 8, scale_rows, 0)
    top_rows, bottom_rows = pl.ds(BASE, HALO), pl.ds(BASE + TR - HALO, HALO)
    top_halo, bottom_halo = pl.ds(BASE - HALO, HALO), pl.ds(BASE + TR, HALO)
    own = pl.ds(BASE, TR)
    tile = pl.ds(0, NB)

    def pair(ref, cols, ss, rs_):
        cps = [
            remote(ref.at[:, cols, bottom_rows, :], ref.at[:, cols, top_halo, :], ss.at[0], rs_.at[0], (down, c)),
            remote(ref.at[:, cols, top_rows, :], ref.at[:, cols, bottom_halo, :], ss.at[1], rs_.at[1], (up, c)),
        ]
        for cp in cps:
            cp.start()
        return cps

    row_cp = pair(X, tile, row_ss, row_rs)

    lane64 = iota((64, LANES), 1)
    quarter = TR // 4

    def packed(ref, k, block, shift):
        parts = [
            pltpu.roll(ref[k, block, pl.ds(BASE + q * quarter, quarter), :], (32 * q + shift) % LANES, 1)
            for q in range(4)
        ]
        return jnp.where(
            lane64 < 64, jnp.where(lane64 < 32, parts[0], parts[1]), jnp.where(lane64 < 96, parts[2], parts[3])
        )

    def unpacked(from_right, from_left, q):
        a, b = from_right, from_left
        if q:
            a = pltpu.roll(a, LANES - 32 * q, 1)
        if q != 3:
            b = pltpu.roll(b, 96 - 32 * q, 1)
        return jnp.where(lane64 < 64, a, b)

    for k in range(NX):
        pack_l[k] = packed(X, k, 0, 0)
        pack_r[k] = packed(X, k, NB - 1, 32)
    col_cp = [
        remote(pack_l, got_r, col_ss.at[0], col_rs.at[0], (r, left)),
        remote(pack_r, got_l, col_ss.at[1], col_rs.at[1], (r, right)),
    ]
    for cp in col_cp:
        cp.start()

    for cp in panel_cp:
        cp.wait()
    at = lax.rem(c * per_tile, 8)
    upper = iota((STRIPE, LANES), 0) < PANEL_ROWS

    def choose(f, to):
        first = panel_r[to, pl.ds(at, 1), :]
        second = panel_r[to, pl.ds(at + 1, 1), :]
        res = []
        for b in range(NB):
            cols = pl.ds(pl.multiple_of(to * (NB * LANES) + b * LANES, LANES), LANES)
            p = jnp.where(
                upper,
                jnp.broadcast_to(first[:, b : b + 1], (STRIPE, LANES)),
                jnp.broadcast_to(second[:, b : b + 1], (STRIPE, LANES)),
            )
            x = rain_v[f, 0, :, cols].astype(jnp.float32)
            for s in range(1, SOURCES):
                x = jnp.where(p == s, rain_v[f, s, :, cols].astype(jnp.float32), x)
            res.append(x.astype(jnp.bfloat16))
        return res

    my_rows = pl.ds(pl.multiple_of(c * STRIPE, STRIPE), STRIPE)

    def rain_copy(f, o):
        to = lax.rem(c + o, NCOL)
        return remote(rs.at[f, to], rx.at[f, :, my_rows, :], rain_ss.at[f, o], rain_rs.at[f, o], (r, to))

    def send_rain(f):
        def one(o, _):
            to = lax.rem(c + o, NCOL)
            for b, x in enumerate(choose(f, to)):
                rs[f, to, b] = x
            rain_copy(f, o).start()
            return 0

        lax.fori_loop(1, NCOL, one, 0)
        for b, x in enumerate(choose(f, c)):
            rx[f, b, my_rows, :] = x

    in_rain[0].wait()
    send_rain(0)

    for cp in ga_cp:
        cp.wait()
    half = iota((8, LANES), 0) < CAP
    lane8 = iota((8, LANES), 1)
    cc = jnp.zeros((8, LANES), jnp.float32)
    for k in range(NCOL):
        cc = cc + jnp.where(lane8 // CAP == k, ga_r[k, 8 + per : 16 + per, :], 0.0)
    for q in range(NR):
        for p in range(NCOL // 2):
            lo8 = ga_r[2 * p, pl.ds(8 + CAP * q, 8), :]
            hi8 = ga_r[2 * p + 1, pl.ds(8 - CAP + CAP * q, 8), :]
            gb[q, p * 8 : p * 8 + 8, :] = jnp.where(half, lo8, hi8)
        gb[q, NCOL * CAP : NCOL * CAP + 8, :] = jnp.broadcast_to(cc[q : q + 1], (8, LANES))
    gb_cp = []
    for o in range(1, NR):
        to = lax.rem(r + o, NR)
        cp = remote(gb.at[to], gb_r.at[r], gb_ss.at[o], gb_rs.at[o], (to, c))
        cp.start()
        gb_cp.append(cp)
    gb_r[r] = gb[r]

    for cp in col_cp:
        cp.wait()
    inside = ((lane64 < 32) & (c < NCOL - 1)) | ((lane64 >= 96) & (c > 0))
    for k in range(NX):
        for q in range(4):
            x = unpacked(got_r[k], got_l[k], q)
            if k == 4:
                x = jnp.where(inside, x, 0.0)
            X[k, NB, pl.ds(BASE + q * quarter, quarter), :] = x
    row8_cp = pair(X, pl.ds(NB, 1), row8_ss, row8_rs)

    in_rain[1].wait()
    send_rain(1)

    for cp in gb_cp:
        cp.wait()
    pieces = []
    for k in range(0, NR, 2):
        a = gb_r[k, NCOL * CAP : NCOL * CAP + 1, :]
        b = pltpu.roll(gb_r[k + 1, NCOL * CAP : NCOL * CAP + 8, :], 64, 1)[0:1]
        pieces.append(jnp.where(iota((1, LANES), 1) < 64, a, b))
    cell_row = jnp.concatenate(pieces, axis=1)
    got = split3(jnp.concatenate([gb_r[k, 0 : NCOL * CAP, :] for k in range(NR)], axis=0))

    def fill(b, _):
        at_cell = (iota((TR, slots), 0) * NB + b).astype(jnp.float32)
        hot = jnp.where(at_cell == cell_row, 1.0, 0.0).astype(jnp.bfloat16)
        SG[b] = join3(dot(hot, got))
        return 0

    lax.fori_loop(0, NB, fill, 0)

    for cp in row_cp + row8_cp:
        cp.wait()
    zero = jnp.zeros((8, LANES), jnp.float32)
    for k in range(NX):
        for b in range(NB + 1):
            X[k, b, 0:8, :] = zero
            X[k, b, RP - 8 : RP, :] = zero

    @pl.when(r == 0)
    def _():
        for b in range(NB + 1):
            X[4, b, top_halo, :] = jnp.zeros((HALO, LANES), jnp.float32)

    @pl.when(r == NR - 1)
    def _():
        for b in range(NB + 1):
            X[4, b, bottom_halo, :] = jnp.zeros((HALO, LANES), jnp.float32)

    last = lane8 == LANES - 1
    first = lane8 == 0

    def eastward(xs):
        ro = [pltpu.roll(x, LANES - 1, 1) for x in xs]
        return [jnp.where(last, ro[(b + 1) % (NB + 1)], ro[b]) for b in range(NB + 1)]

    def prepare(i, _):
        rows = pl.ds(mul8(i), 8)
        south = pl.ds(mul8(i) + 1, 8)
        zs = [X[3, b, rows, :] for b in range(NB + 1)]
        ns = [X[4, b, rows, :] for b in range(NB + 1)]
        ze, ne = eastward(zs), eastward(ns)
        en = eastward([X[0, b, rows, :] for b in range(NB + 1)])
        for b in range(NB + 1):
            EN[b, rows, :] = en[b]
            for zn, nn, Z, F, B in (
                (ze[b], ne[b], ZE, FE, BE),
                (X[3, b, south, :], X[4, b, south, :], ZS, FS, BS),
            ):
                Z[b, rows, :] = jnp.maximum(zs[b], zn)
                n = jnp.abs(ns[b]) + jnp.abs(nn)
                F[b, rows, :] = FRIC * (n * n)
                B[b, rows, :] = jnp.where(jnp.minimum(ns[b], nn) > 0.0, 1.0, jnp.inf)
        return 0

    lax.fori_loop(0, RP // 8 - 1, prepare, 0)

    def scol(f):
        return [
            remote(spack_l.at[f], sgot_r.at[f], scol_ss.at[f, 0], scol_rs.at[f, 0], (r, left)),
            remote(spack_r.at[f], sgot_l.at[f], scol_ss.at[f, 1], scol_rs.at[f, 1], (r, right)),
        ]

    def srow(f, cols, ss, rs_):
        return [
            remote(S.at[f, cols, bottom_rows, :], S.at[f, cols, top_halo, :], ss.at[f, 0], rs_.at[f, 0], (down, c)),
            remote(S.at[f, cols, top_rows, :], S.at[f, cols, bottom_halo, :], ss.at[f, 1], rs_.at[f, 1], (up, c)),
        ]

    def sources1(f):
        def wait_rain(o, _):
            rain_copy(f, o).wait()
            return 0

        lax.fori_loop(1, NCOL, wait_rain, 0)

        def add(i, _):
            rows = pl.ds(pl.multiple_of(i * 16, 16), 16)
            for b in range(NB):
                S[f, b, pl.ds(pl.multiple_of(i * 16 + BASE, 16), 16), :] = SCALE * (
                    rx[f, b, rows, :].astype(jnp.float32) + SG[b, rows, :]
                )
            return 0

        lax.fori_loop(0, TR // 16, add, 0)
        spack_l[f] = packed(S, f, 0, 0)
        spack_r[f] = packed(S, f, NB - 1, 32)
        for cp in scol(f) + srow(f, tile, srow_ss, srow_rs):
            cp.start()

    def sources2(f):
        for cp in scol(f):
            cp.wait()
        for q in range(4):
            S[f, NB, pl.ds(BASE + q * quarter, quarter), :] = unpacked(sgot_r[f], sgot_l[f], q)
        for cp in srow(f, pl.ds(NB, 1), srow8_ss, srow8_rs):
            cp.start()

    def sources3(f):
        for cp in srow(f, tile, srow_ss, srow_rs) + srow(f, pl.ds(NB, 1), srow8_ss, srow8_rs):
            cp.wait()
        for b in range(NB + 1):
            S[f, b, 0:8, :] = zero
            S[f, b, RP - 8 : RP, :] = zero

    sources1(0)
    sources2(0)
    sources3(0)

    def faces(rho):
        rows = pl.ds(rho, 8)
        for b in range(NB + 1):
            eta = X[0, b, rows, :]
            X[1, b, rows, :] = face(eta, EN[b, rows, :], X[1, b, rows, :], ZE[b, rows, :], FE[b, rows, :], BE[b, rows, :])
            X[2, b, rows, :] = face(
                eta, X[0, b, pl.ds(rho + 1, 8), :], X[2, b, rows, :], ZS[b, rows, :], FS[b, rows, :], BS[b, rows, :]
            )

    def update(f, rho):
        rows = pl.ds(rho, 8)
        qe = [X[1, b, rows, :] for b in range(NB + 1)]
        ro = [pltpu.roll(x, 1, 1) for x in qe]
        eta = []
        for b in range(NB + 1):
            west = jnp.where(first, ro[(b - 1) % (NB + 1)], ro[b])
            x = (
                X[0, b, rows, :]
                + ((west - qe[b]) + (X[2, b, pl.ds(rho - 1, 8), :] - X[2, b, rows, :]))
                + S[f, b, rows, :]
            )
            eta.append(x)
            X[0, b, rows, :] = x
        for b, x in enumerate(eastward(eta)):
            EN[b, rows, :] = x

    def step(t, _):
        @pl.when(t == 2)
        def _():
            sources1(1)

        @pl.when(t == 5)
        def _():
            sources2(1)

        @pl.when(t == STEPS // FRAMES)
        def _():
            sources3(1)

        f = t * FRAMES // STEPS
        m = STEPS - 1 - t
        lo = BASE // 8 - (m // 8 + 1)
        hi = (BASE + TR) // 8 + (m + 7) // 8
        hi = hi + lax.rem(hi - lo, 2)
        big = (hi - lo) // 6

        def six(i, _):
            for k in range(6):
                rho = mul8(lo + i * 6 + k)
                faces(rho)
                update(f, rho)
            return 0

        def two(i, _):
            for k in range(2):
                rho = mul8(lo + big * 6 + i * 2 + k)
                faces(rho)
                update(f, rho)
            return 0

        lax.fori_loop(0, big, six, 0)
        lax.fori_loop(0, (hi - lo - big * 6) // 2, two, 0)
        return 0

    lax.fori_loop(0, STEPS, step, 0)

    def finish(i, _):
        rows = pl.ds(mul8(i), 8)
        at_ = pl.ds(mul8(i + BASE // 8), 8)
        for b in range(NB):
            cols = pl.ds(b * LANES, LANES)
            outs[0, rows, cols] = (X[0, b, at_, :] - X[3, b, at_, :]) * (1.0 / SCALE)
            outs[1, rows, cols] = X[1, b, at_, :] * (1.0 / QSCALE)
            outs[2, rows, cols] = X[2, b, at_, :] * (1.0 / QSCALE)
        return 0

    lax.fori_loop(0, TR // 8, finish, 0)
    done = [local(outs.at[0], out_h, 12), local(outs.at[1], out_e, 13), local(outs.at[2], out_s, 14)]
    for cp in done:
        cp.wait()


def body(depth, flow_e, flow_s, elev, rough, wet, rain, panel, inflow, gtile, gcell):
    f32, bf16, i32 = jnp.float32, jnp.bfloat16, jnp.int32
    dma = pltpu.SemaphoreType.DMA
    rows, cols = depth.shape
    per = NR * CAP
    ext = pltpu.VMEM((NB + 1, RP, LANES), f32)
    scratch = [
        pltpu.VMEM((NX, rows, cols), f32),
        pltpu.VMEM((rows, cols), i32),
        pltpu.VMEM(rain.shape, bf16),
        pltpu.VMEM(panel.shape, i32),
        pltpu.VMEM(inflow.shape, f32),
        pltpu.VMEM(gtile.shape, i32),
        pltpu.VMEM((GD // LANES, LANES), i32),
        pltpu.VMEM((NX, NB + 1, RP, LANES), f32),
        ext, ext, ext, ext, ext, ext, ext,
        pltpu.VMEM((FRAMES, NB + 1, RP, LANES), f32),
        pltpu.VMEM((NB, rows, LANES), f32),
        pltpu.VMEM((NCOL, 8, panel.shape[1]), i32),
        pltpu.VMEM((NCOL, per + 16, LANES), f32),
        pltpu.VMEM((NCOL, per + 16, LANES), f32),
        pltpu.VMEM((NR, NCOL * CAP + 8, LANES), f32),
        pltpu.VMEM((NR, NCOL * CAP + 8, LANES), f32),
        pltpu.VMEM((FRAMES, NCOL, NB, STRIPE, LANES), bf16),
        pltpu.VMEM((FRAMES, NB, rows, LANES), bf16),
        *([pltpu.VMEM((NX, rows // 4, LANES), f32)] * 4),
        *([pltpu.VMEM((FRAMES, rows // 4, LANES), f32)] * 4),
        pltpu.VMEM((3, rows, cols), f32),
        dma((15,)),
        dma((NCOL,)), dma((NCOL,)),
        dma((NCOL,)), dma((NCOL,)),
        dma((NR,)), dma((NR,)),
        dma((FRAMES, NCOL)), dma((FRAMES, NCOL)),
        dma((2,)), dma((2,)),
        dma((2,)), dma((2,)),
        dma((2,)), dma((2,)),
        dma((FRAMES, 2)), dma((FRAMES, 2)),
        dma((FRAMES, 2)), dma((FRAMES, 2)),
        dma((FRAMES, 2)), dma((FRAMES, 2)),
    ]
    out = jax.ShapeDtypeStruct(depth.shape, f32)
    hbm = pl.BlockSpec(memory_space=pl.ANY)
    return pl.pallas_call(
        kernel,
        out_shape=(out, out, out),
        in_specs=[hbm] * 11,
        out_specs=(hbm, hbm, hbm),
        scratch_shapes=scratch,
        compiler_params=pltpu.CompilerParams(
            collective_id=0, has_side_effects=True, vmem_limit_bytes=60 * 1024 * 1024
        ),
        name="inundation",
    )(depth, flow_e, flow_s, elev, rough, wet, rain, panel, inflow, gtile, gcell.reshape(GD // LANES, LANES))


def solution(mesh):
    placed = (
        P("row", "col"),
        P("row", "col"),
        P("row", "col"),
        P("row", "col"),
        P("row", "col"),
        P("row", "col"),
        P(None, None, ("row", "col"), None),
        P("row", "col"),
        P(("row", "col"), None),
        P(("row", "col"), None),
        P(("row", "col")),
    )
    return jax.shard_map(
        body,
        mesh=mesh,
        in_specs=placed,
        out_specs=(P("row", "col"), P("row", "col"), P("row", "col")),
        check_vma=False,
    )
```

```python
import functools

import jax
import jax.numpy as jnp
from jax import lax
from jax.experimental import pallas as pl
from jax.experimental.pallas import tpu as pltpu
from jax.sharding import PartitionSpec as P

STEPS = 20
FRAMES = 2
SOURCES = 3
PANEL_ROWS = 8
LANES = 128
CAP = 4
NR = 8
NCOL = 16
TR = 256
NB = 8
HALO = 8
BASE = 16
RP = BASE + TR + 16
SPAN = 7
MID = tuple(range(SPAN, STEPS, SPAN))
STRIPE = TR // NCOL
GD = 256
NX = 5

GRAVITY = 9.81
DT = 5.0
DX = 90.0
RATIO = DT / DX
SCALE = RATIO * GRAVITY * DT / DX
QSCALE = SCALE * RATIO
FLOOR = 0.1 * SCALE
FRIC = GRAVITY * DT * 0.25 * SCALE ** (7.0 / 3.0) / QSCALE
VMEM_LIMIT = 60 * 1024 * 1024
PART = 128
MESH = pl.DeviceIdType.MESH


def split3(x):
    hi = x.astype(jnp.bfloat16)
    rest = x - hi.astype(jnp.float32)
    mid = rest.astype(jnp.bfloat16)
    low = (rest - mid.astype(jnp.float32)).astype(jnp.bfloat16)
    return jnp.concatenate([hi, mid, low], axis=1)


def join3(x):
    return (x[:, :LANES] + x[:, LANES : 2 * LANES]) + x[:, 2 * LANES :]


def dot(a, b):
    return lax.dot_general(a, b, (((1,), (0,)), ((), ())), preferred_element_type=jnp.float32)


def iota(shape, axis):
    return lax.broadcasted_iota(jnp.int32, shape, axis)


def face(eta, nxt, q, zmax, fric, base):
    hf = jnp.maximum(jnp.maximum(eta, nxt) - zmax, FLOOR)
    drv = q - hf * (nxt - eta)
    pw = jnp.exp2(jnp.log2(hf) * (-7.0 / 3.0))
    return drv * (1.0 / (base + jnp.abs(q) * fric * pw))


def mul8(x):
    return pl.multiple_of(x * 8, 8)


def kernel(
    depth, flow_e, flow_s, elev, rough, wet, rain, panel, inflow, gtile, gcell,
    out,
    stage, wet_v, rain_v, panel_v, inflow_v, gtile_v, gcell_v,
    X, ZE, ZS, FE, FS, BE, BS, EN, S, SG,
    panel_r, ga, ga_r, gb, gb_r, rs, rx, pack_l, pack_r, got_l, got_r, spack_l, spack_r, sgot_l, sgot_r, corner, scorner, mid_out, mid_in,
    loc, panel_ss, panel_rs, ga_ss, ga_rs, gb_ss, gb_rs, rain_ss, rain_rs,
    halo_ss, halo_rs, shalo_ss, shalo_rs, mid_ss, mid_rs,
):
    r = lax.axis_index("row")
    c = lax.axis_index("col")
    up, down = lax.rem(r + NR - 1, NR), lax.rem(r + 1, NR)
    left, right = lax.rem(c + NCOL - 1, NCOL), lax.rem(c + 1, NCOL)

    def local(src, dst, k):
        cp = pltpu.make_async_copy(src, dst, loc.at[k])
        cp.start()
        return cp

    def remote(src, dst, ss, rs_, dev):
        return pltpu.make_async_remote_copy(
            src_ref=src, dst_ref=dst, send_sem=ss, recv_sem=rs_, device_id=dev, device_id_type=MESH
        )

    in_panel = local(panel, panel_v, 0)
    in_gauge = [local(inflow, inflow_v, 1), local(gtile, gtile_v, 2), local(gcell, gcell_v, 3)]
    in_tile = [
        local(depth, stage.at[0], 4),
        local(flow_e, stage.at[1], 5),
        local(flow_s, stage.at[2], 6),
        local(elev, stage.at[3], 7),
        local(rough, stage.at[4], 8),
        local(wet, wet_v, 9),
    ]
    in_rain = [local(rain.at[f], rain_v.at[f], 10 + f) for f in range(FRAMES)]

    barrier = pltpu.get_barrier_semaphore()
    partners = [(r, lax.rem(c + o, NCOL)) for o in range(1, NCOL)]
    partners += [(lax.rem(r + o, NR), c) for o in range(1, NR)]
    partners += [(v, h) for v in (up, down) for h in (left, right)]
    for dev in partners:
        pl.semaphore_signal(barrier, inc=1, device_id=dev, device_id_type=MESH)

    for cp in in_gauge:
        cp.wait()
    g0, g1 = iota((GD, GD), 0), iota((GD, GD), 1)
    eye = g0 == g1

    def as_row(ref):
        return jnp.concatenate([ref[k : k + 1, :] for k in range(GD // LANES)], axis=1).astype(jnp.float32)

    def as_col(row):
        return jnp.sum(jnp.where(eye, row, 0.0), axis=1, keepdims=True)

    tile_row = as_row(gtile_v)
    same = as_col(tile_row) == tile_row
    rank_col = jnp.sum(jnp.where(same & (g1 < g0), 1.0, 0.0), axis=1, keepdims=True)
    rank_row = jnp.sum(jnp.where(same & (g0 < g1), 1.0, 0.0), axis=0, keepdims=True)
    tile_r = jnp.floor(tile_row * (1.0 / NCOL))
    tile_c = tile_row - tile_r * NCOL
    place = tile_c * NR + tile_r
    slot = place * CAP + rank_row
    slots = NR * NCOL * CAP
    pick = jnp.where(iota((slots, GD), 0).astype(jnp.float32) == slot, 1.0, 0.0).astype(jnp.bfloat16)
    vals = join3(dot(pick, split3(inflow_v[...])))
    cell_col = as_col(as_row(gcell_v))
    cell_hi = jnp.floor(cell_col * 0.125)
    cell_lo = cell_col - cell_hi * 8.0
    mine = rank_col == lax.rem(iota((GD, LANES), 1), CAP).astype(jnp.float32)
    cell_x = jnp.concatenate([jnp.where(mine, cell_hi, 0.0), jnp.where(mine, cell_lo, 0.0)], axis=1)
    order = iota((NR * NCOL, GD), 0).astype(jnp.float32) == place
    cell_y = dot(jnp.where(order, 1.0, 0.0).astype(jnp.bfloat16), cell_x.astype(jnp.bfloat16))
    cell_t = cell_y[:, :LANES] * 8.0 + cell_y[:, LANES:]
    per = NR * CAP
    for k in range(NCOL):
        ga[k, 8 : 8 + per, :] = vals[k * per : (k + 1) * per]
        ga[k, 8 + per : 16 + per, :] = cell_t[k * NR : (k + 1) * NR]

    for cp in in_tile:
        cp.wait()

    def scale_rows(i, _):
        rows = pl.ds(mul8(i), 8)
        to = pl.ds(mul8(i + BASE // 8), 8)
        for b in range(NB):
            cols = pl.ds(b * LANES, LANES)
            z = stage[3, rows, cols] * SCALE
            X[0, b, to, :] = stage[0, rows, cols] * SCALE + z
            X[1, b, to, :] = stage[1, rows, cols] * QSCALE
            X[2, b, to, :] = stage[2, rows, cols] * QSCALE
            X[3, b, to, :] = z
            n = stage[4, rows, cols]
            X[4, b, to, :] = jnp.where(wet_v[rows, cols] > 0, n, -n)
        return 0

    lax.fori_loop(0, TR // 8, scale_rows, 0)
    top_rows, bottom_rows = pl.ds(BASE, HALO), pl.ds(BASE + TR - HALO, HALO)
    top_halo, bottom_halo = pl.ds(BASE - HALO, HALO), pl.ds(BASE + TR, HALO)
    tile = pl.ds(0, NB)
    quarter = TR // 4
    lane_h = iota((quarter, LANES), 1)
    ends = pl.ds(0, HALO), pl.ds(quarter - HALO, HALO)

    def packed(ref, k, block, shift):
        parts = [
            pltpu.roll(ref[k, block, pl.ds(BASE + q * quarter, quarter), :], (32 * q + shift) % LANES, 1)
            for q in range(4)
        ]
        return jnp.where(
            lane_h < 64, jnp.where(lane_h < 32, parts[0], parts[1]), jnp.where(lane_h < 96, parts[2], parts[3])
        )

    def unpacked(from_right, from_left, q):
        a, b = from_right, from_left
        if q:
            a = pltpu.roll(a, LANES - 32 * q, 1)
        if q != 3:
            b = pltpu.roll(b, 96 - 32 * q, 1)
        return jnp.where(iota(a.shape, 1) < 64, a, b)

    for k in range(NX):
        pack_l[k] = packed(X, k, 0, 0)
        pack_r[k] = packed(X, k, NB - 1, 32)

    in_panel.wait()
    pl.semaphore_wait(barrier, len(partners))

    panel_cp, ga_cp = [], []
    for o in range(1, NCOL):
        to = lax.rem(c + o, NCOL)
        cp = remote(panel_v, panel_r.at[c], panel_ss.at[o], panel_rs.at[o], (r, to))
        cp.start()
        panel_cp.append(cp)
    hop = pl.ds(8, per + 8)
    for o in range(1, NCOL):
        to = lax.rem(c + o, NCOL)
        cp = remote(ga.at[to, hop], ga_r.at[c, hop], ga_ss.at[o], ga_rs.at[o], (r, to))
        cp.start()
        ga_cp.append(cp)
    panel_r[c] = panel_v[...]
    ga_r[c, hop, :] = ga[c, hop, :]

    has_up, has_down, has_left, has_right = r > 0, r < NR - 1, c > 0, c < NCOL - 1

    def row_copies(ref, ss, rs_):
        return [
            (remote(ref.at[:, tile, bottom_rows, :], ref.at[:, tile, top_halo, :], ss(0), rs_(0), (down, c)),
             has_down, has_up),
            (remote(ref.at[:, tile, top_rows, :], ref.at[:, tile, bottom_halo, :], ss(1), rs_(1), (up, c)),
             has_up, has_down),
        ]

    def col_copies(pl_, pr_, gl, gr, cn, ss, rs_):
        return [
            (remote(pl_, gr, ss(2), rs_(2), (r, left)), has_left, has_right),
            (remote(pr_, gl, ss(3), rs_(3), (r, right)), has_right, has_left),
            (remote(pl_.at[:, ends[1], :], cn.at[0], ss(4), rs_(4), (down, left)),
             has_down & has_left, has_up & has_right),
            (remote(pr_.at[:, ends[1], :], cn.at[1], ss(5), rs_(5), (down, right)),
             has_down & has_right, has_up & has_left),
            (remote(pl_.at[:, ends[0], :], cn.at[2], ss(6), rs_(6), (up, left)),
             has_up & has_left, has_down & has_right),
            (remote(pr_.at[:, ends[0], :], cn.at[3], ss(7), rs_(7), (up, right)),
             has_up & has_right, has_down & has_left),
        ]

    def start_all(copies):
        for cp, sends, _ in copies:
            pl.when(sends)(cp.start)

    def wait_sent(copies):
        for cp, sends, _ in copies:
            pl.when(sends)(cp.wait_send)

    def wait_got(copies):
        for cp, _, gets in copies:
            pl.when(gets)(cp.wait_recv)

    def wait_all(copies):
        wait_sent(copies)
        wait_got(copies)

    def beside(x):
        lane = iota(x.shape, 1)
        return jnp.where(((lane < 32) & has_right) | ((lane >= 96) & has_left), x, 0.0)

    def clear_border(ref, k):
        @pl.when(r == 0)
        def _():
            for b in range(NB + 1):
                ref[k, b, top_halo, :] = jnp.zeros((HALO, LANES), jnp.float32)

        @pl.when(r == NR - 1)
        def _():
            for b in range(NB + 1):
                ref[k, b, bottom_halo, :] = jnp.zeros((HALO, LANES), jnp.float32)

    sem = lambda ref: (lambda k: ref.at[k])
    row_cp = row_copies(X, sem(halo_ss), sem(halo_rs))
    col_cp = col_copies(pack_l, pack_r, got_l, got_r, corner, sem(halo_ss), sem(halo_rs))
    start_all(col_cp + row_cp)

    for cp in panel_cp:
        cp.wait()
    at = c * (STRIPE // PANEL_ROWS)
    upper = iota((STRIPE, LANES), 0) < PANEL_ROWS

    def choose(f, to):
        x = panel_r[to].astype(jnp.float32)
        lane_p = iota(x.shape, 1)
        first = jnp.sum(jnp.where(lane_p == at, x, 0.0), axis=1, keepdims=True)
        second = jnp.sum(jnp.where(lane_p == at + 1, x, 0.0), axis=1, keepdims=True)
        res = []
        for b in range(NB):
            cols = pl.ds(pl.multiple_of(to * (NB * LANES) + b * LANES, LANES), LANES)
            p = jnp.where(
                upper,
                jnp.broadcast_to(first[b : b + 1], (STRIPE, LANES)),
                jnp.broadcast_to(second[b : b + 1], (STRIPE, LANES)),
            )
            x = rain_v[f, 0, :, cols].astype(jnp.float32)
            for s in range(1, SOURCES):
                x = jnp.where(p == s, rain_v[f, s, :, cols].astype(jnp.float32), x)
            res.append(x.astype(jnp.bfloat16))
        return res

    my_rows = pl.ds(pl.multiple_of(c * STRIPE, STRIPE), STRIPE)

    def rain_copy(f, o):
        to = lax.rem(c + o, NCOL)
        return remote(rs.at[f, to], rx.at[f, :, my_rows, :], rain_ss.at[f, o], rain_rs.at[f, o], (r, to))

    def choose_rain(f, send):
        in_rain[f].wait()

        def one(o, _):
            to = lax.rem(c + o, NCOL)
            for b, x in enumerate(choose(f, to)):
                rs[f, to, b] = x
            if send:
                rain_copy(f, o).start()
            return 0

        lax.fori_loop(1, NCOL, one, 0)
        for b, x in enumerate(choose(f, c)):
            rx[f, b, my_rows, :] = x

    choose_rain(0, True)

    for cp in ga_cp:
        cp.wait()
    half = iota((8, LANES), 0) < CAP
    lane8 = iota((8, LANES), 1)
    cc = jnp.zeros((8, LANES), jnp.float32)
    for k in range(NCOL):
        cc = cc + jnp.where(lane8 // CAP == k, ga_r[k, 8 + per : 16 + per, :], 0.0)
    for q in range(NR):
        for p in range(NCOL // 2):
            lo8 = ga_r[2 * p, pl.ds(8 + CAP * q, 8), :]
            hi8 = ga_r[2 * p + 1, pl.ds(8 - CAP + CAP * q, 8), :]
            gb[q, p * 8 : p * 8 + 8, :] = jnp.where(half, lo8, hi8)
        gb[q, NCOL * CAP : NCOL * CAP + 8, :] = jnp.broadcast_to(cc[q : q + 1], (8, LANES))
    gb_cp = []
    for o in range(1, NR):
        to = lax.rem(r + o, NR)
        cp = remote(gb.at[to], gb_r.at[r], gb_ss.at[o], gb_rs.at[o], (to, c))
        cp.start()
        gb_cp.append(cp)
    gb_r[r] = gb[r]

    wait_all(col_cp)

    zero = jnp.zeros((8, LANES), jnp.float32)
    for k in range(NX):
        for q in range(4):
            X[k, NB, pl.ds(BASE + q * quarter, quarter), :] = beside(unpacked(got_r[k], got_l[k], q))
        for b in range(NB + 1):
            X[k, b, 0:8, :] = zero
            X[k, b, RP - 8 : RP, :] = zero

    last = lane8 == LANES - 1
    first = lane8 == 0

    def eastward(xs):
        ro = [pltpu.roll(x, LANES - 1, 1) for x in xs]
        return [jnp.where(last, ro[(b + 1) % (NB + 1)], ro[b]) for b in range(NB + 1)]

    def prepare(i):
        rows = pl.ds(mul8(i), 8)
        south = pl.ds(mul8(i) + 1, 8)
        zs = [X[3, b, rows, :] for b in range(NB + 1)]
        ns = [X[4, b, rows, :] for b in range(NB + 1)]
        ze, ne = eastward(zs), eastward(ns)
        en = eastward([X[0, b, rows, :] for b in range(NB + 1)])
        for b in range(NB + 1):
            EN[b, rows, :] = en[b]
            for zn, nn, Z, F, B in (
                (ze[b], ne[b], ZE, FE, BE),
                (X[3, b, south, :], X[4, b, south, :], ZS, FS, BS),
            ):
                Z[b, rows, :] = jnp.maximum(zs[b], zn)
                n = jnp.abs(ns[b]) + jnp.abs(nn)
                F[b, rows, :] = FRIC * (n * n)
                B[b, rows, :] = jnp.where(jnp.minimum(ns[b], nn) > 0.0, 1.0, jnp.inf)

    own_lo, own_hi = BASE // 8, (BASE + TR) // 8

    def prepare_own(i, _):
        prepare(i)
        return 0

    lax.fori_loop(own_lo, own_hi - 1, prepare_own, 0)

    for cp in gb_cp:
        cp.wait()
    pieces = []
    for k in range(0, NR, 2):
        a = gb_r[k, NCOL * CAP : NCOL * CAP + 1, :]
        b = pltpu.roll(gb_r[k + 1, NCOL * CAP : NCOL * CAP + 8, :], 64, 1)[0:1]
        pieces.append(jnp.where(iota((1, LANES), 1) < 64, a, b))
    cell_row = jnp.concatenate(pieces, axis=1)
    got = split3(jnp.concatenate([gb_r[k, 0 : NCOL * CAP, :] for k in range(NR)], axis=0))

    def fill(b, _):
        at_cell = (iota((TR, slots), 0) * NB + b).astype(jnp.float32)
        hot = jnp.where(at_cell == cell_row, 1.0, 0.0).astype(jnp.bfloat16)
        SG[b] = join3(dot(hot, got))
        return 0

    lax.fori_loop(0, NB, fill, 0)

    def source_rows(f):
        frame = pl.ds(f, 1)
        return row_copies(S.at[frame], lambda k: shalo_ss.at[f, k], lambda k: shalo_rs.at[f, k])

    def source_cols(f):
        frame = pl.ds(f, 1)
        return col_copies(
            spack_l.at[frame], spack_r.at[frame], sgot_l.at[frame], sgot_r.at[frame], scorner.at[f],
            lambda k: shalo_ss.at[f, k], lambda k: shalo_rs.at[f, k],
        )

    def sources_out(f):
        def wait_rain(o, _):
            rain_copy(f, o).wait()
            return 0

        lax.fori_loop(1, NCOL, wait_rain, 0)

        def add(i, _):
            rows = pl.ds(pl.multiple_of(i * 16, 16), 16)
            for b in range(NB):
                S[f, b, pl.ds(pl.multiple_of(i * 16 + BASE, 16), 16), :] = SCALE * (
                    rx[f, b, rows, :].astype(jnp.float32) + SG[b, rows, :]
                )
            return 0

        lax.fori_loop(0, TR // 16, add, 0)
        spack_l[f] = packed(S, f, 0, 0)
        spack_r[f] = packed(S, f, NB - 1, 32)
        start_all(source_cols(f) + source_rows(f))
        for b in range(NB + 1):
            S[f, b, 0:8, :] = zero
            S[f, b, RP - 8 : RP, :] = zero

    def sources_in(f):
        wait_all(source_cols(f) + source_rows(f))
        for q in range(4):
            S[f, NB, pl.ds(BASE + q * quarter, quarter), :] = beside(unpacked(sgot_r[f], sgot_l[f], q))
        S[f, NB, top_halo, :] = beside(unpacked(scorner[f, 0, 0], scorner[f, 1, 0], 3))
        S[f, NB, bottom_halo, :] = beside(unpacked(scorner[f, 2, 0], scorner[f, 3, 0], 0))
        clear_border(S, f)

    sources_out(0)

    choose_rain(1, True)

    def halos_in():
        wait_got(row_cp)
        for k in range(NX):
            X[k, NB, top_halo, :] = beside(unpacked(corner[0, k], corner[1, k], 3))
            X[k, NB, bottom_halo, :] = beside(unpacked(corner[2, k], corner[3, k], 0))
            clear_border(X, k)

        def prepare_halo(i, _):
            prepare(jnp.where(i == 0, own_lo - 1, own_hi - 2 + i))
            return 0

        lax.fori_loop(0, 3, prepare_halo, 0)

    def mid_copies(e):
        return [
            (remote(mid_out.at[e, 0], mid_in.at[e, 0], mid_ss.at[e, 0], mid_rs.at[e, 0], (down, c)), has_down, has_up),
            (remote(mid_out.at[e, 1], mid_in.at[e, 1], mid_ss.at[e, 1], mid_rs.at[e, 1], (up, c)), has_up, has_down),
        ]

    def mid_send(e):
        for k in range(3):
            for b in range(NB + 1):
                mid_out[e, 0, k, b] = X[k, b, bottom_rows, :]
                mid_out[e, 1, k, b] = X[k, b, top_rows, :]
        start_all(mid_copies(e))

    def mid_take(e):
        wait_all(mid_copies(e))
        for side, here, has in ((0, top_halo, has_up), (1, bottom_halo, has_down)):

            @pl.when(has)
            def _():
                for k in range(3):
                    for b in range(NB + 1):
                        X[k, b, here, :] = mid_in[e, side, k, b]
                for b, x in enumerate(eastward([mid_in[e, side, 0, b] for b in range(NB + 1)])):
                    EN[b, here, :] = x

    def faces(rho):
        rows = pl.ds(rho, 8)
        for b in range(NB + 1):
            eta = X[0, b, rows, :]
            X[1, b, rows, :] = face(eta, EN[b, rows, :], X[1, b, rows, :], ZE[b, rows, :], FE[b, rows, :], BE[b, rows, :])
            X[2, b, rows, :] = face(
                eta, X[0, b, pl.ds(rho + 1, 8), :], X[2, b, rows, :], ZS[b, rows, :], FS[b, rows, :], BS[b, rows, :]
            )

    def update(f, rho):
        rows = pl.ds(rho, 8)
        qe = [X[1, b, rows, :] for b in range(NB + 1)]
        ro = [pltpu.roll(x, 1, 1) for x in qe]
        eta = []
        for b in range(NB + 1):
            west = jnp.where(first, ro[(b - 1) % (NB + 1)], ro[b])
            x = (
                X[0, b, rows, :]
                + ((west - qe[b]) + (X[2, b, pl.ds(rho - 1, 8), :] - X[2, b, rows, :]))
                + S[f, b, rows, :]
            )
            eta.append(x)
            X[0, b, rows, :] = x
        for b, x in enumerate(eastward(eta)):
            EN[b, rows, :] = x

    def blocks(count, start, do):
        def run(i, _):
            for k in range(count):
                do(mul8(start + i * count + k))
            return 0

        return run

    lo, hi = own_lo - 1, own_hi + 1

    def step(t, _):
        f = t * FRAMES // STEPS

        @pl.when(t == 5)
        def _():
            sources_out(1)

        @pl.when(t == STEPS // FRAMES)
        def _():
            sources_in(1)

        def both(rho):
            faces(rho)
            update(f, rho)

        def only_update(rho):
            update(f, rho)

        def split(arrive):
            lax.fori_loop(0, 6, blocks(5, own_lo, faces), 0)
            arrive()
            for i in (lo, own_hi - 2, own_hi - 1, own_hi):
                faces(i * 8)
            if arrive is first_halos:
                sources_in(0)
            lax.fori_loop(0, 8, blocks(4, lo, only_update), 0)
            for i in (hi - 2, hi - 1):
                update(f, i * 8)

        def boundary_first(e):
            top, bottom = own_lo, own_hi - 1
            for i in (top - 1, top, top + 1, bottom - 1, bottom, bottom + 1):
                faces(i * 8)
            update(f, top * 8)
            update(f, bottom * 8)
            mid_send(e)
            lax.fori_loop(0, 7, blocks(4, top + 2, faces), 0)
            for i in (top - 1, bottom + 1):
                update(f, i * 8)
            lax.fori_loop(0, 7, blocks(4, top + 1, only_update), 0)
            for i in (bottom - 2, bottom - 1):
                update(f, i * 8)

        first_halos = halos_in

        @pl.when(t == 0)
        def _():
            wait_sent(row_cp)
            split(first_halos)

        for e, at_t in enumerate(MID):

            @pl.when(t == at_t)
            def _():
                split(functools.partial(mid_take, e))

        @pl.when((lax.rem(t, SPAN) != 0) & ((lax.rem(t, SPAN) != SPAN - 1) | (t > MID[-1])))
        def _():
            lax.fori_loop(0, 5, blocks(6, lo, both), 0)
            lax.fori_loop(0, 1, blocks(4, lo + 30, both), 0)

        for e, at_t in enumerate(MID):

            @pl.when(t == at_t - 1)
            def _():
                boundary_first(e)

        return 0

    lax.fori_loop(0, STEPS, step, 0)

    def depth_rows(i, _):
        rows = pl.ds(mul8(i), 8)
        for b in range(NB):
            X[0, b, rows, :] = X[0, b, rows, :] - X[3, b, rows, :]
        return 0

    done = [local(X.at[k, tile, pl.ds(BASE, TR), :], out.at[k], 12 + k) for k in (1, 2)]
    lax.fori_loop(own_lo, own_hi, depth_rows, 0)
    done.append(local(X.at[0, tile, pl.ds(BASE, TR), :], out.at[0], 12))
    for cp in done:
        cp.wait()


def finish(x, out_h, out_e, out_s):
    for b in range(NB):
        cols = slice(b * LANES, (b + 1) * LANES)
        out_h[:, cols] = x[0, b] * (1.0 / SCALE)
        out_e[:, cols] = x[1, b] * (1.0 / QSCALE)
        out_s[:, cols] = x[2, b] * (1.0 / QSCALE)


def body(depth, flow_e, flow_s, elev, rough, wet, rain, panel, inflow, gtile, gcell):
    f32, bf16, i32 = jnp.float32, jnp.bfloat16, jnp.int32
    dma = pltpu.SemaphoreType.DMA
    rows, cols = depth.shape
    ext = pltpu.VMEM((NB + 1, RP, LANES), f32)
    scratch = [
        pltpu.VMEM((NX, rows, cols), f32),
        pltpu.VMEM((rows, cols), i32),
        pltpu.VMEM(rain.shape, bf16),
        pltpu.VMEM(panel.shape[::-1], i32),
        pltpu.VMEM(inflow.shape, f32),
        pltpu.VMEM((GD // LANES, LANES), i32),
        pltpu.VMEM((GD // LANES, LANES), i32),
        pltpu.VMEM((NX, NB + 1, RP, LANES), f32),
        ext, ext, ext, ext, ext, ext, ext,
        pltpu.VMEM((FRAMES, NB + 1, RP, LANES), f32),
        pltpu.VMEM((NB, rows, LANES), f32),
        pltpu.VMEM((NCOL, *panel.shape[::-1]), i32),
        pltpu.VMEM((NCOL, NR * CAP + 16, LANES), f32),
        pltpu.VMEM((NCOL, NR * CAP + 16, LANES), f32),
        pltpu.VMEM((NR, NCOL * CAP + 8, LANES), f32),
        pltpu.VMEM((NR, NCOL * CAP + 8, LANES), f32),
        pltpu.VMEM((FRAMES, NCOL, NB, STRIPE, LANES), bf16),
        pltpu.VMEM((FRAMES, NB, rows, LANES), bf16),
        *([pltpu.VMEM((NX, rows // 4, LANES), f32)] * 4),
        *([pltpu.VMEM((FRAMES, rows // 4, LANES), f32)] * 4),
        pltpu.VMEM((4, NX, HALO, LANES), f32),
        pltpu.VMEM((FRAMES, 4, 1, HALO, LANES), f32),
        *([pltpu.VMEM((len(MID), 2, 3, NB + 1, HALO, LANES), f32)] * 2),
        dma((16,)),
        dma((NCOL,)), dma((NCOL,)),
        dma((NCOL,)), dma((NCOL,)),
        dma((NR,)), dma((NR,)),
        dma((FRAMES, NCOL)), dma((FRAMES, NCOL)),
        dma((8,)), dma((8,)),
        dma((FRAMES, 8)), dma((FRAMES, 8)),
        dma((len(MID), 2)), dma((len(MID), 2)),
    ]
    hbm = pl.BlockSpec(memory_space=pl.ANY)
    state = pl.pallas_call(
        kernel,
        out_shape=jax.ShapeDtypeStruct((3, NB, rows, LANES), f32),
        in_specs=[hbm] * 11,
        out_specs=hbm,
        scratch_shapes=scratch,
        compiler_params=pltpu.CompilerParams(
            collective_id=0, has_side_effects=True, vmem_limit_bytes=VMEM_LIMIT
        ),
        name="inundation",
    )(
        depth, flow_e, flow_s, elev, rough, wet, rain, panel.T, inflow,
        gtile.reshape(GD // LANES, LANES), gcell.reshape(GD // LANES, LANES),
    )
    part = PART
    out = jax.ShapeDtypeStruct(depth.shape, f32)
    return pl.pallas_call(
        finish,
        grid=(rows // part,),
        out_shape=(out, out, out),
        in_specs=[pl.BlockSpec((3, NB, part, LANES), lambda i: (0, 0, i, 0))],
        out_specs=[pl.BlockSpec((part, cols), lambda i: (i, 0))] * 3,
        compiler_params=pltpu.CompilerParams(vmem_limit_bytes=VMEM_LIMIT),
        name="unscale",
    )(state)


def solution(mesh):
    placed = (
        P("row", "col"),
        P("row", "col"),
        P("row", "col"),
        P("row", "col"),
        P("row", "col"),
        P("row", "col"),
        P(None, None, ("row", "col"), None),
        P("row", "col"),
        P(("row", "col"), None),
        P(("row", "col"), None),
        P(("row", "col")),
    )
    return jax.shard_map(
        body,
        mesh=mesh,
        in_specs=placed,
        out_specs=(P("row", "col"), P("row", "col"), P("row", "col")),
        check_vma=False,
    )
```

```python
import functools

import jax
import jax.numpy as jnp
from jax import lax
from jax.experimental import pallas as pl
from jax.experimental.pallas import tpu as pltpu
from jax.sharding import PartitionSpec as P

STEPS = 20
FRAMES = 2
SOURCES = 3
PANEL_ROWS = 8
LANES = 128
CAP = 4
NR = 8
NCOL = 16
TR = 256
NB = 8
HALO = 8
BASE = 16
RP = BASE + TR + 16
SPAN = 7
MID = tuple(range(SPAN, STEPS, SPAN))
STRIPE = TR // NCOL
GD = 256
NX = 5

GRAVITY = 9.81
DT = 5.0
DX = 90.0
RATIO = DT / DX
SCALE = RATIO * GRAVITY * DT / DX
QSCALE = SCALE * RATIO
FLOOR = 0.1 * SCALE
FRIC = GRAVITY * DT * 0.25 * SCALE ** (7.0 / 3.0) / QSCALE
VMEM_LIMIT = 60 * 1024 * 1024
PART = 128
MESH = pl.DeviceIdType.MESH


def split3(x):
    hi = x.astype(jnp.bfloat16)
    rest = x - hi.astype(jnp.float32)
    mid = rest.astype(jnp.bfloat16)
    low = (rest - mid.astype(jnp.float32)).astype(jnp.bfloat16)
    return jnp.concatenate([hi, mid, low], axis=1)


def join3(x):
    return (x[:, :LANES] + x[:, LANES : 2 * LANES]) + x[:, 2 * LANES :]


def dot(a, b):
    return lax.dot_general(a, b, (((1,), (0,)), ((), ())), preferred_element_type=jnp.float32)


def iota(shape, axis):
    return lax.broadcasted_iota(jnp.int32, shape, axis)


def face(eta, nxt, q, zmax, fric, base):
    hf = jnp.maximum(jnp.maximum(eta, nxt) - zmax, FLOOR)
    drv = q - hf * (nxt - eta)
    pw = jnp.exp2(jnp.log2(hf) * (-7.0 / 3.0))
    return drv * (1.0 / (base + jnp.abs(q) * fric * pw))


def mul8(x):
    return pl.multiple_of(x * 8, 8)


def kernel(
    depth, flow_e, flow_s, elev, rough, wet, rain, panel, inflow, gtile, gcell,
    out,
    stage, wet_v, rain_v, panel_v, inflow_v, gtile_v, gcell_v,
    X, ZE, ZS, FE, FS, BE, BS, EN, S, SG,
    panel_r, ga, ga_r, gb, gb_r, rs, rx, pack_l, pack_r, got_l, got_r, spack_l, spack_r, sgot_l, sgot_r, corner, scorner, mid_out, mid_in,
    loc, panel_ss, panel_rs, ga_ss, ga_rs, gb_ss, gb_rs, rain_ss, rain_rs,
    halo_ss, halo_rs, shalo_ss, shalo_rs, mid_ss, mid_rs,
):
    r = lax.axis_index("row")
    c = lax.axis_index("col")
    up, down = lax.rem(r + NR - 1, NR), lax.rem(r + 1, NR)
    left, right = lax.rem(c + NCOL - 1, NCOL), lax.rem(c + 1, NCOL)

    def local(src, dst, k):
        cp = pltpu.make_async_copy(src, dst, loc.at[k])
        cp.start()
        return cp

    def remote(src, dst, ss, rs_, dev):
        return pltpu.make_async_remote_copy(
            src_ref=src, dst_ref=dst, send_sem=ss, recv_sem=rs_, device_id=dev, device_id_type=MESH
        )

    in_panel = local(panel, panel_v, 0)
    in_gauge = [local(inflow, inflow_v, 1), local(gtile, gtile_v, 2), local(gcell, gcell_v, 3)]
    in_tile = [
        local(depth, stage.at[0], 4),
        local(flow_e, stage.at[1], 5),
        local(flow_s, stage.at[2], 6),
        local(elev, stage.at[3], 7),
        local(rough, stage.at[4], 8),
        local(wet, wet_v, 9),
    ]
    in_rain = [local(rain.at[f], rain_v.at[f], 10 + f) for f in range(FRAMES)]

    barrier = pltpu.get_barrier_semaphore()
    partners = [(r, lax.rem(c + o, NCOL)) for o in range(1, NCOL)]
    partners += [(lax.rem(r + o, NR), c) for o in range(1, NR)]
    partners += [(v, h) for v in (up, down) for h in (left, right)]
    for dev in partners:
        pl.semaphore_signal(barrier, inc=1, device_id=dev, device_id_type=MESH)

    in_panel.wait()
    pl.semaphore_wait(barrier, len(partners))

    panel_cp, ga_cp = [], []
    for o in range(1, NCOL):
        to = lax.rem(c + o, NCOL)
        cp = remote(panel_v, panel_r.at[c], panel_ss.at[o], panel_rs.at[o], (r, to))
        cp.start()
        panel_cp.append(cp)
    panel_r[c] = panel_v[...]

    for cp in in_gauge:
        cp.wait()
    g0, g1 = iota((GD, GD), 0), iota((GD, GD), 1)
    eye = g0 == g1

    def as_row(ref):
        return jnp.concatenate([ref[k : k + 1, :] for k in range(GD // LANES)], axis=1).astype(jnp.float32)

    def as_col(row):
        return jnp.sum(jnp.where(eye, row, 0.0), axis=1, keepdims=True)

    tile_row = as_row(gtile_v)
    same = as_col(tile_row) == tile_row
    rank_col = jnp.sum(jnp.where(same & (g1 < g0), 1.0, 0.0), axis=1, keepdims=True)
    rank_row = jnp.sum(jnp.where(same & (g0 < g1), 1.0, 0.0), axis=0, keepdims=True)
    tile_r = jnp.floor(tile_row * (1.0 / NCOL))
    tile_c = tile_row - tile_r * NCOL
    place = tile_c * NR + tile_r
    slot = place * CAP + rank_row
    slots = NR * NCOL * CAP
    pick = jnp.where(iota((slots, GD), 0).astype(jnp.float32) == slot, 1.0, 0.0).astype(jnp.bfloat16)
    vals = join3(dot(pick, split3(inflow_v[...])))
    cell_col = as_col(as_row(gcell_v))
    cell_hi = jnp.floor(cell_col * 0.125)
    cell_lo = cell_col - cell_hi * 8.0
    mine = rank_col == lax.rem(iota((GD, LANES), 1), CAP).astype(jnp.float32)
    cell_x = jnp.concatenate([jnp.where(mine, cell_hi, 0.0), jnp.where(mine, cell_lo, 0.0)], axis=1)
    order = iota((NR * NCOL, GD), 0).astype(jnp.float32) == place
    cell_y = dot(jnp.where(order, 1.0, 0.0).astype(jnp.bfloat16), cell_x.astype(jnp.bfloat16))
    cell_t = cell_y[:, :LANES] * 8.0 + cell_y[:, LANES:]
    per = NR * CAP
    for k in range(NCOL):
        ga[k, 8 : 8 + per, :] = vals[k * per : (k + 1) * per]
        ga[k, 8 + per : 16 + per, :] = cell_t[k * NR : (k + 1) * NR]

    hop = pl.ds(8, per + 8)
    for o in range(1, NCOL):
        to = lax.rem(c + o, NCOL)
        cp = remote(ga.at[to, hop], ga_r.at[c, hop], ga_ss.at[o], ga_rs.at[o], (r, to))
        cp.start()
        ga_cp.append(cp)
    ga_r[c, hop, :] = ga[c, hop, :]

    for cp in in_tile:
        cp.wait()

    def scale_rows(i, _):
        rows = pl.ds(mul8(i), 8)
        to = pl.ds(mul8(i + BASE // 8), 8)
        for b in range(NB):
            cols = pl.ds(b * LANES, LANES)
            z = stage[3, rows, cols] * SCALE
            X[0, b, to, :] = stage[0, rows, cols] * SCALE + z
            X[1, b, to, :] = stage[1, rows, cols] * QSCALE
            X[2, b, to, :] = stage[2, rows, cols] * QSCALE
            X[3, b, to, :] = z
            n = stage[4, rows, cols]
            X[4, b, to, :] = jnp.where(wet_v[rows, cols] > 0, n, -n)
        return 0

    lax.fori_loop(0, TR // 8, scale_rows, 0)
    top_rows, bottom_rows = pl.ds(BASE, HALO), pl.ds(BASE + TR - HALO, HALO)
    top_halo, bottom_halo = pl.ds(BASE - HALO, HALO), pl.ds(BASE + TR, HALO)
    tile = pl.ds(0, NB)
    quarter = TR // 4
    lane_h = iota((quarter, LANES), 1)
    ends = pl.ds(0, HALO), pl.ds(quarter - HALO, HALO)

    def packed(ref, k, block, shift):
        parts = [
            pltpu.roll(ref[k, block, pl.ds(BASE + q * quarter, quarter), :], (32 * q + shift) % LANES, 1)
            for q in range(4)
        ]
        return jnp.where(
            lane_h < 64, jnp.where(lane_h < 32, parts[0], parts[1]), jnp.where(lane_h < 96, parts[2], parts[3])
        )

    def unpacked(from_right, from_left, q):
        a, b = from_right, from_left
        if q:
            a = pltpu.roll(a, LANES - 32 * q, 1)
        if q != 3:
            b = pltpu.roll(b, 96 - 32 * q, 1)
        return jnp.where(iota(a.shape, 1) < 64, a, b)

    for k in range(NX):
        pack_l[k] = packed(X, k, 0, 0)
        pack_r[k] = packed(X, k, NB - 1, 32)

    has_up, has_down, has_left, has_right = r > 0, r < NR - 1, c > 0, c < NCOL - 1

    def row_copies(ref, ss, rs_):
        return [
            (remote(ref.at[:, tile, bottom_rows, :], ref.at[:, tile, top_halo, :], ss(0), rs_(0), (down, c)),
             has_down, has_up),
            (remote(ref.at[:, tile, top_rows, :], ref.at[:, tile, bottom_halo, :], ss(1), rs_(1), (up, c)),
             has_up, has_down),
        ]

    def col_copies(pl_, pr_, gl, gr, cn, ss, rs_):
        return [
            (remote(pl_, gr, ss(2), rs_(2), (r, left)), has_left, has_right),
            (remote(pr_, gl, ss(3), rs_(3), (r, right)), has_right, has_left),
            (remote(pl_.at[:, ends[1], :], cn.at[0], ss(4), rs_(4), (down, left)),
             has_down & has_left, has_up & has_right),
            (remote(pr_.at[:, ends[1], :], cn.at[1], ss(5), rs_(5), (down, right)),
             has_down & has_right, has_up & has_left),
            (remote(pl_.at[:, ends[0], :], cn.at[2], ss(6), rs_(6), (up, left)),
             has_up & has_left, has_down & has_right),
            (remote(pr_.at[:, ends[0], :], cn.at[3], ss(7), rs_(7), (up, right)),
             has_up & has_right, has_down & has_left),
        ]

    def start_all(copies):
        for cp, sends, _ in copies:
            pl.when(sends)(cp.start)

    def wait_sent(copies):
        for cp, sends, _ in copies:
            pl.when(sends)(cp.wait_send)

    def wait_got(copies):
        for cp, _, gets in copies:
            pl.when(gets)(cp.wait_recv)

    def wait_all(copies):
        wait_sent(copies)
        wait_got(copies)

    def beside(x):
        lane = iota(x.shape, 1)
        return jnp.where(((lane < 32) & has_right) | ((lane >= 96) & has_left), x, 0.0)

    def clear_border(ref, k):
        @pl.when(r == 0)
        def _():
            for b in range(NB + 1):
                ref[k, b, top_halo, :] = jnp.zeros((HALO, LANES), jnp.float32)

        @pl.when(r == NR - 1)
        def _():
            for b in range(NB + 1):
                ref[k, b, bottom_halo, :] = jnp.zeros((HALO, LANES), jnp.float32)

    sem = lambda ref: (lambda k: ref.at[k])
    row_cp = row_copies(X, sem(halo_ss), sem(halo_rs))
    col_cp = col_copies(pack_l, pack_r, got_l, got_r, corner, sem(halo_ss), sem(halo_rs))
    start_all(col_cp + row_cp)

    for cp in panel_cp:
        cp.wait()
    at = c * (STRIPE // PANEL_ROWS)
    upper = iota((STRIPE, LANES), 0) < PANEL_ROWS

    def choose(f, to):
        x = panel_r[to].astype(jnp.float32)
        lane_p = iota(x.shape, 1)
        first = jnp.sum(jnp.where(lane_p == at, x, 0.0), axis=1, keepdims=True)
        second = jnp.sum(jnp.where(lane_p == at + 1, x, 0.0), axis=1, keepdims=True)
        res = []
        for b in range(NB):
            cols = pl.ds(pl.multiple_of(to * (NB * LANES) + b * LANES, LANES), LANES)
            p = jnp.where(
                upper,
                jnp.broadcast_to(first[b : b + 1], (STRIPE, LANES)),
                jnp.broadcast_to(second[b : b + 1], (STRIPE, LANES)),
            )
            x = rain_v[f, 0, :, cols].astype(jnp.float32)
            for s in range(1, SOURCES):
                x = jnp.where(p == s, rain_v[f, s, :, cols].astype(jnp.float32), x)
            res.append(x.astype(jnp.bfloat16))
        return res

    my_rows = pl.ds(pl.multiple_of(c * STRIPE, STRIPE), STRIPE)

    def rain_copy(f, o):
        to = lax.rem(c + o, NCOL)
        return remote(rs.at[f, to], rx.at[f, :, my_rows, :], rain_ss.at[f, o], rain_rs.at[f, o], (r, to))

    def choose_rain(f, send):
        in_rain[f].wait()

        def one(o, _):
            to = lax.rem(c + o, NCOL)
            for b, x in enumerate(choose(f, to)):
                rs[f, to, b] = x
            if send:
                rain_copy(f, o).start()
            return 0

        lax.fori_loop(1, NCOL, one, 0)
        for b, x in enumerate(choose(f, c)):
            rx[f, b, my_rows, :] = x

    choose_rain(0, True)

    for cp in ga_cp:
        cp.wait()
    half = iota((8, LANES), 0) < CAP
    lane8 = iota((8, LANES), 1)
    cc = jnp.zeros((8, LANES), jnp.float32)
    for k in range(NCOL):
        cc = cc + jnp.where(lane8 // CAP == k, ga_r[k, 8 + per : 16 + per, :], 0.0)
    for q in range(NR):
        for p in range(NCOL // 2):
            lo8 = ga_r[2 * p, pl.ds(8 + CAP * q, 8), :]
            hi8 = ga_r[2 * p + 1, pl.ds(8 - CAP + CAP * q, 8), :]
            gb[q, p * 8 : p * 8 + 8, :] = jnp.where(half, lo8, hi8)
        gb[q, NCOL * CAP : NCOL * CAP + 8, :] = jnp.broadcast_to(cc[q : q + 1], (8, LANES))
    gb_cp = []
    for o in range(1, NR):
        to = lax.rem(r + o, NR)
        cp = remote(gb.at[to], gb_r.at[r], gb_ss.at[o], gb_rs.at[o], (to, c))
        cp.start()
        gb_cp.append(cp)
    gb_r[r] = gb[r]

    wait_all(col_cp)

    zero = jnp.zeros((8, LANES), jnp.float32)
    for k in range(NX):
        for q in range(4):
            X[k, NB, pl.ds(BASE + q * quarter, quarter), :] = beside(unpacked(got_r[k], got_l[k], q))
        for b in range(NB + 1):
            X[k, b, 0:8, :] = zero
            X[k, b, RP - 8 : RP, :] = zero

    last = lane8 == LANES - 1
    first = lane8 == 0

    def eastward(xs):
        ro = [pltpu.roll(x, LANES - 1, 1) for x in xs]
        return [jnp.where(last, ro[(b + 1) % (NB + 1)], ro[b]) for b in range(NB + 1)]

    def prepare(i):
        rows = pl.ds(mul8(i), 8)
        south = pl.ds(mul8(i) + 1, 8)
        zs = [X[3, b, rows, :] for b in range(NB + 1)]
        ns = [X[4, b, rows, :] for b in range(NB + 1)]
        ze, ne = eastward(zs), eastward(ns)
        en = eastward([X[0, b, rows, :] for b in range(NB + 1)])
        for b in range(NB + 1):
            EN[b, rows, :] = en[b]
            for zn, nn, Z, F, B in (
                (ze[b], ne[b], ZE, FE, BE),
                (X[3, b, south, :], X[4, b, south, :], ZS, FS, BS),
            ):
                Z[b, rows, :] = jnp.maximum(zs[b], zn)
                n = jnp.abs(ns[b]) + jnp.abs(nn)
                F[b, rows, :] = FRIC * (n * n)
                B[b, rows, :] = jnp.where(jnp.minimum(ns[b], nn) > 0.0, 1.0, jnp.inf)

    own_lo, own_hi = BASE // 8, (BASE + TR) // 8

    def prepare_own(i, _):
        prepare(i)
        return 0

    lax.fori_loop(own_lo, own_hi - 1, prepare_own, 0)

    for cp in gb_cp:
        cp.wait()
    pieces = []
    for k in range(0, NR, 2):
        a = gb_r[k, NCOL * CAP : NCOL * CAP + 1, :]
        b = pltpu.roll(gb_r[k + 1, NCOL * CAP : NCOL * CAP + 8, :], 64, 1)[0:1]
        pieces.append(jnp.where(iota((1, LANES), 1) < 64, a, b))
    cell_row = jnp.concatenate(pieces, axis=1)
    got = split3(jnp.concatenate([gb_r[k, 0 : NCOL * CAP, :] for k in range(NR)], axis=0))

    def fill(b, _):
        at_cell = (iota((TR, slots), 0) * NB + b).astype(jnp.float32)
        hot = jnp.where(at_cell == cell_row, 1.0, 0.0).astype(jnp.bfloat16)
        SG[b] = join3(dot(hot, got))
        return 0

    lax.fori_loop(0, NB, fill, 0)

    def source_rows(f):
        frame = pl.ds(f, 1)
        return row_copies(S.at[frame], lambda k: shalo_ss.at[f, k], lambda k: shalo_rs.at[f, k])

    def source_cols(f):
        frame = pl.ds(f, 1)
        return col_copies(
            spack_l.at[frame], spack_r.at[frame], sgot_l.at[frame], sgot_r.at[frame], scorner.at[f],
            lambda k: shalo_ss.at[f, k], lambda k: shalo_rs.at[f, k],
        )

    def sources_out(f):
        def wait_rain(o, _):
            rain_copy(f, o).wait()
            return 0

        lax.fori_loop(1, NCOL, wait_rain, 0)

        def add(i, _):
            rows = pl.ds(pl.multiple_of(i * 16, 16), 16)
            for b in range(NB):
                S[f, b, pl.ds(pl.multiple_of(i * 16 + BASE, 16), 16), :] = SCALE * (
                    rx[f, b, rows, :].astype(jnp.float32) + SG[b, rows, :]
                )
            return 0

        lax.fori_loop(0, TR // 16, add, 0)
        spack_l[f] = packed(S, f, 0, 0)
        spack_r[f] = packed(S, f, NB - 1, 32)
        start_all(source_cols(f) + source_rows(f))
        for b in range(NB + 1):
            S[f, b, 0:8, :] = zero
            S[f, b, RP - 8 : RP, :] = zero

    def sources_in(f):
        wait_all(source_cols(f) + source_rows(f))
        for q in range(4):
            S[f, NB, pl.ds(BASE + q * quarter, quarter), :] = beside(unpacked(sgot_r[f], sgot_l[f], q))
        S[f, NB, top_halo, :] = beside(unpacked(scorner[f, 0, 0], scorner[f, 1, 0], 3))
        S[f, NB, bottom_halo, :] = beside(unpacked(scorner[f, 2, 0], scorner[f, 3, 0], 0))
        clear_border(S, f)

    sources_out(0)

    choose_rain(1, True)

    def halos_in():
        wait_got(row_cp)
        for k in range(NX):
            X[k, NB, top_halo, :] = beside(unpacked(corner[0, k], corner[1, k], 3))
            X[k, NB, bottom_halo, :] = beside(unpacked(corner[2, k], corner[3, k], 0))
            clear_border(X, k)

        def prepare_halo(i, _):
            prepare(jnp.where(i == 0, own_lo - 1, own_hi - 2 + i))
            return 0

        lax.fori_loop(0, 3, prepare_halo, 0)

    def mid_copies(e):
        return [
            (remote(mid_out.at[e, 0], mid_in.at[e, 0], mid_ss.at[e, 0], mid_rs.at[e, 0], (down, c)), has_down, has_up),
            (remote(mid_out.at[e, 1], mid_in.at[e, 1], mid_ss.at[e, 1], mid_rs.at[e, 1], (up, c)), has_up, has_down),
        ]

    def mid_send(e):
        for k in range(3):
            for b in range(NB + 1):
                mid_out[e, 0, k, b] = X[k, b, bottom_rows, :]
                mid_out[e, 1, k, b] = X[k, b, top_rows, :]
        start_all(mid_copies(e))

    def mid_take(e):
        wait_all(mid_copies(e))
        for side, here, has in ((0, top_halo, has_up), (1, bottom_halo, has_down)):

            @pl.when(has)
            def _():
                for k in range(3):
                    for b in range(NB + 1):
                        X[k, b, here, :] = mid_in[e, side, k, b]
                for b, x in enumerate(eastward([mid_in[e, side, 0, b] for b in range(NB + 1)])):
                    EN[b, here, :] = x

    def faces(rho):
        rows = pl.ds(rho, 8)
        for b in range(NB + 1):
            eta = X[0, b, rows, :]
            X[1, b, rows, :] = face(eta, EN[b, rows, :], X[1, b, rows, :], ZE[b, rows, :], FE[b, rows, :], BE[b, rows, :])
            X[2, b, rows, :] = face(
                eta, X[0, b, pl.ds(rho + 1, 8), :], X[2, b, rows, :], ZS[b, rows, :], FS[b, rows, :], BS[b, rows, :]
            )

    def update(f, rho):
        rows = pl.ds(rho, 8)
        qe = [X[1, b, rows, :] for b in range(NB + 1)]
        ro = [pltpu.roll(x, 1, 1) for x in qe]
        eta = []
        for b in range(NB + 1):
            west = jnp.where(first, ro[(b - 1) % (NB + 1)], ro[b])
            x = (
                X[0, b, rows, :]
                + ((west - qe[b]) + (X[2, b, pl.ds(rho - 1, 8), :] - X[2, b, rows, :]))
                + S[f, b, rows, :]
            )
            eta.append(x)
            X[0, b, rows, :] = x
        for b, x in enumerate(eastward(eta)):
            EN[b, rows, :] = x

    def blocks(count, start, do):
        def run(i, _):
            for k in range(count):
                do(mul8(start + i * count + k))
            return 0

        return run

    lo, hi = own_lo - 1, own_hi + 1

    def step(t, _):
        f = t * FRAMES // STEPS

        @pl.when(t == 5)
        def _():
            sources_out(1)

        @pl.when(t == STEPS // FRAMES)
        def _():
            sources_in(1)

        def both(rho):
            faces(rho)
            update(f, rho)

        def only_update(rho):
            update(f, rho)

        def split(arrive):
            lax.fori_loop(0, 6, blocks(5, own_lo, faces), 0)
            arrive()
            for i in (lo, own_hi - 2, own_hi - 1, own_hi):
                faces(i * 8)
            if arrive is first_halos:
                sources_in(0)
            lax.fori_loop(0, 8, blocks(4, lo, only_update), 0)
            for i in (hi - 2, hi - 1):
                update(f, i * 8)

        def boundary_first(e):
            top, bottom = own_lo, own_hi - 1
            for i in (top - 1, top, top + 1, bottom - 1, bottom, bottom + 1):
                faces(i * 8)
            update(f, top * 8)
            update(f, bottom * 8)
            mid_send(e)
            lax.fori_loop(0, 7, blocks(4, top + 2, faces), 0)
            for i in (top - 1, bottom + 1):
                update(f, i * 8)
            lax.fori_loop(0, 7, blocks(4, top + 1, only_update), 0)
            for i in (bottom - 2, bottom - 1):
                update(f, i * 8)

        first_halos = halos_in

        @pl.when(t == 0)
        def _():
            wait_sent(row_cp)
            split(first_halos)

        for e, at_t in enumerate(MID):

            @pl.when(t == at_t)
            def _():
                split(functools.partial(mid_take, e))

        @pl.when((lax.rem(t, SPAN) != 0) & ((lax.rem(t, SPAN) != SPAN - 1) | (t > MID[-1])))
        def _():
            lax.fori_loop(0, 5, blocks(6, lo, both), 0)
            lax.fori_loop(0, 1, blocks(4, lo + 30, both), 0)

        for e, at_t in enumerate(MID):

            @pl.when(t == at_t - 1)
            def _():
                boundary_first(e)

        return 0

    lax.fori_loop(0, STEPS, step, 0)

    def depth_rows(i, _):
        rows = pl.ds(mul8(i), 8)
        for b in range(NB):
            X[0, b, rows, :] = X[0, b, rows, :] - X[3, b, rows, :]
        return 0

    done = [local(X.at[k, tile, pl.ds(BASE, TR), :], out.at[k], 12 + k) for k in (1, 2)]
    lax.fori_loop(own_lo, own_hi, depth_rows, 0)
    done.append(local(X.at[0, tile, pl.ds(BASE, TR), :], out.at[0], 12))
    for cp in done:
        cp.wait()


def finish(x, out_h, out_e, out_s):
    for b in range(NB):
        cols = slice(b * LANES, (b + 1) * LANES)
        out_h[:, cols] = x[0, b] * (1.0 / SCALE)
        out_e[:, cols] = x[1, b] * (1.0 / QSCALE)
        out_s[:, cols] = x[2, b] * (1.0 / QSCALE)


def body(depth, flow_e, flow_s, elev, rough, wet, rain, panel, inflow, gtile, gcell):
    f32, bf16, i32 = jnp.float32, jnp.bfloat16, jnp.int32
    dma = pltpu.SemaphoreType.DMA
    rows, cols = depth.shape
    ext = pltpu.VMEM((NB + 1, RP, LANES), f32)
    scratch = [
        pltpu.VMEM((NX, rows, cols), f32),
        pltpu.VMEM((rows, cols), i32),
        pltpu.VMEM(rain.shape, bf16),
        pltpu.VMEM(panel.shape[::-1], i32),
        pltpu.VMEM(inflow.shape, f32),
        pltpu.VMEM((GD // LANES, LANES), i32),
        pltpu.VMEM((GD // LANES, LANES), i32),
        pltpu.VMEM((NX, NB + 1, RP, LANES), f32),
        ext, ext, ext, ext, ext, ext, ext,
        pltpu.VMEM((FRAMES, NB + 1, RP, LANES), f32),
        pltpu.VMEM((NB, rows, LANES), f32),
        pltpu.VMEM((NCOL, *panel.shape[::-1]), i32),
        pltpu.VMEM((NCOL, NR * CAP + 16, LANES), f32),
        pltpu.VMEM((NCOL, NR * CAP + 16, LANES), f32),
        pltpu.VMEM((NR, NCOL * CAP + 8, LANES), f32),
        pltpu.VMEM((NR, NCOL * CAP + 8, LANES), f32),
        pltpu.VMEM((FRAMES, NCOL, NB, STRIPE, LANES), bf16),
        pltpu.VMEM((FRAMES, NB, rows, LANES), bf16),
        *([pltpu.VMEM((NX, rows // 4, LANES), f32)] * 4),
        *([pltpu.VMEM((FRAMES, rows // 4, LANES), f32)] * 4),
        pltpu.VMEM((4, NX, HALO, LANES), f32),
        pltpu.VMEM((FRAMES, 4, 1, HALO, LANES), f32),
        *([pltpu.VMEM((len(MID), 2, 3, NB + 1, HALO, LANES), f32)] * 2),
        dma((16,)),
        dma((NCOL,)), dma((NCOL,)),
        dma((NCOL,)), dma((NCOL,)),
        dma((NR,)), dma((NR,)),
        dma((FRAMES, NCOL)), dma((FRAMES, NCOL)),
        dma((8,)), dma((8,)),
        dma((FRAMES, 8)), dma((FRAMES, 8)),
        dma((len(MID), 2)), dma((len(MID), 2)),
    ]
    hbm = pl.BlockSpec(memory_space=pl.ANY)
    state = pl.pallas_call(
        kernel,
        out_shape=jax.ShapeDtypeStruct((3, NB, rows, LANES), f32),
        in_specs=[hbm] * 11,
        out_specs=hbm,
        scratch_shapes=scratch,
        compiler_params=pltpu.CompilerParams(
            collective_id=0, has_side_effects=True, vmem_limit_bytes=VMEM_LIMIT
        ),
        name="inundation",
    )(
        depth, flow_e, flow_s, elev, rough, wet, rain, panel.T, inflow,
        gtile.reshape(GD // LANES, LANES), gcell.reshape(GD // LANES, LANES),
    )
    part = PART
    out = jax.ShapeDtypeStruct(depth.shape, f32)
    return pl.pallas_call(
        finish,
        grid=(rows // part,),
        out_shape=(out, out, out),
        in_specs=[pl.BlockSpec((3, NB, part, LANES), lambda i: (0, 0, i, 0))],
        out_specs=[pl.BlockSpec((part, cols), lambda i: (i, 0))] * 3,
        compiler_params=pltpu.CompilerParams(vmem_limit_bytes=VMEM_LIMIT),
        name="unscale",
    )(state)


def solution(mesh):
    placed = (
        P("row", "col"),
        P("row", "col"),
        P("row", "col"),
        P("row", "col"),
        P("row", "col"),
        P("row", "col"),
        P(None, None, ("row", "col"), None),
        P("row", "col"),
        P(("row", "col"), None),
        P(("row", "col"), None),
        P(("row", "col")),
    )
    return jax.shard_map(
        body,
        mesh=mesh,
        in_specs=placed,
        out_specs=(P("row", "col"), P("row", "col"), P("row", "col")),
        check_vma=False,
    )
```
